32 devices in a mesh: alpha: 8 (over y, x, core), beta: 4 (over z).
Axes of the slice: x: 2, y: 2, z: 4, core: 2. Of those that a mesh axis runs over, the one named last changes fastest.
Arguments:
- coeffs: bfloat16 [256, 512], P('alpha', 'beta'), may hold values from -6 to 6
- integrals: bfloat16 [400, 400], replicated, may hold values from -0.014953613 to 0.014953613
- source_beta: int32 [400, 512], P(None, 'beta'), may hold values from 0 to 511
- sign_beta: int32 [400, 512], P(None, 'beta'), may hold values from -1 to 1
- target_alpha: int32 [256, 400], P('alpha'), may hold values from 0 to 255
- sign_alpha: int32 [256, 400], P('alpha'), may hold values from -1 to 1
Outputs:
- sigma: float32 [256, 512], P('alpha', 'beta')
The draws below stay inside these ranges and needn't reach their ends.
All inputs are finite; a program needn't handle non-finite values.
Results may differ from the reference program's by a relative error of at most 0.0029.
Values may be sent and summed in bfloat16 or wider, within the bound.
A program may use at most 64 MiB of HBM per device.

```python
import jax
import jax.numpy as jnp
from jax import lax

NPAIR = 400
STR_A_DEV = 32
NA = 256
NB = 512


def place_ends(values, key, least, top_value):
    place = [jax.random.randint(jax.random.fold_in(key, axis), (), 0, length) for axis, length in enumerate(values.shape)]
    widest = values.shape.index(max(values.shape))
    next_to = place[:widest] + [(place[widest] + 1) % values.shape[widest]] + place[widest + 1:]
    return values.at[tuple(place)].set(least).at[tuple(next_to)].set(top_value)


def block_levels(stream_key, extent, shards, smallest, top_value):
    gain = 1.0
    for position, blocks in shards:
        heights = jax.random.uniform(jax.random.fold_in(jax.random.fold_in(stream_key, 6), position), (blocks,), jnp.float32, smallest / len(shards), top_value / len(shards))
        gain = gain * jnp.repeat(jnp.exp(heights), extent[position] // blocks).reshape((-1,) + (1,) * (len(extent) - 1 - position))
    return gain


def centred(key, dims, scale, most, shards=(), held_as=jnp.bfloat16):
    drawn = jax.random.normal(key, dims, jnp.float32) * scale
    if len(shards) > 0:
        drawn = block_levels(key, dims, shards, -0.22, 0.18) * drawn
    return jnp.clip(drawn, min=-most, max=most).astype(held_as)


def setup_inputs(seed: int = 0) -> dict:
    keys = jax.random.split(jax.random.key(seed), 7)
    return {
        "coeffs": centred(keys[0], (NA, NB), 1.0, 6.0, ((0, 8), (1, 4))),
        "integrals": centred(keys[1], (NPAIR, NPAIR), (1.0 / NPAIR), 0.014953613),
        "source_beta": place_ends(jax.random.randint(keys[2], (NPAIR, NB), 0, NB), jax.random.fold_in(keys[2], 1), 0, NB - 1).astype(jnp.int32),
        "sign_beta": place_ends(jax.random.randint(keys[3], (NPAIR, NB), -1, 2), jax.random.fold_in(keys[3], 1), -1, 1).astype(jnp.int32),
        "target_alpha": place_ends(jax.random.randint(keys[4], (NA, NPAIR), 0, NA), jax.random.fold_in(keys[4], 1), 0, NA - 1).astype(jnp.int32),
        "sign_alpha": place_ends(jax.random.randint(keys[5], (NA, NPAIR), -1, 2), jax.random.fold_in(keys[5], 1), -1, 1).astype(jnp.int32),
    }


def reference(coeffs, integrals, source_beta, sign_beta, target_alpha, sign_alpha):
    rows_block = STR_A_DEV
    blocks = NA // rows_block
    beta_signs = sign_beta.astype(jnp.bfloat16)
    inter_f = integrals.astype(jnp.float32)

    def step(total, index):
        start = (index * rows_block).astype(jnp.int32)
        rows = lax.dynamic_slice_in_dim(coeffs, start, rows_block, 0)
        excited = rows[:, source_beta] * beta_signs[None, :, :]
        contracted = jnp.einsum("jk,akb->ajb", inter_f, excited.astype(jnp.float32)).astype(jnp.bfloat16)
        targets = lax.dynamic_slice_in_dim(target_alpha, start, rows_block, 0)
        signs = lax.dynamic_slice_in_dim(sign_alpha, start, rows_block, 0).astype(jnp.float32)
        terms = contracted.astype(jnp.float32) * signs[:, :, None]
        flat = terms.reshape(rows_block * NPAIR, NB)
        added = jax.ops.segment_sum(flat, targets.reshape(-1).astype(jnp.int32), num_segments=NA)
        return total + added, None

    total, _ = lax.scan(step, jnp.zeros((NA, NB), jnp.float32), jnp.arange(blocks, dtype=jnp.int32))
    return total
```

```python
import functools

import jax
import jax.numpy as jnp
from jax import lax
from jax.experimental import pallas as pl
from jax.experimental.pallas import tpu as pltpu
from jax.sharding import PartitionSpec as P

MESH = pl.DeviceIdType.MESH
LANES = 128
ROWS = 16


def kernel(
    n_alpha,
    n_beta,
    coeffs_ref,
    integrals_ref,
    source_ref,
    sign_b_ref,
    target_ref,
    sign_a_ref,
    out_ref,
    gathered,
    widened,
    excited,
    table,
    total,
    outgoing,
    incoming,
    gather_send,
    gather_recv,
    sum_send,
    sum_recv,
):
    rows, cols = coeffs_ref.shape
    pairs = integrals_ref.shape[0]
    all_alpha = rows * n_alpha
    ia = lax.axis_index("alpha")
    ib = lax.axis_index("beta")

    barrier = pltpu.get_barrier_semaphore()
    for d in range(1, n_beta):
        pl.semaphore_signal(
            barrier, inc=1, device_id=(ia, lax.rem(ib + d, n_beta)), device_id_type=MESH
        )
    for d in range(1, n_alpha):
        pl.semaphore_signal(
            barrier, inc=1, device_id=(lax.rem(ia + d, n_alpha), ib), device_id_type=MESH
        )
    pl.semaphore_wait(barrier, n_beta + n_alpha - 2)

    gather_copies = []
    for d in range(1, n_beta):
        copy = pltpu.make_async_remote_copy(
            src_ref=coeffs_ref,
            dst_ref=gathered.at[ib],
            send_sem=gather_send.at[d - 1],
            recv_sem=gather_recv.at[d - 1],
            device_id=(ia, lax.rem(ib + d, n_beta)),
            device_id_type=MESH,
        )
        copy.start()
        gather_copies.append(copy)
    gathered[ib] = coeffs_ref[...]

    def build(a, carry):
        targets = target_ref[pl.ds(a, 1), :]
        signs = sign_a_ref[pl.ds(a, 1), :].astype(jnp.float32)
        iota = lax.broadcasted_iota(jnp.int32, (all_alpha, pairs), 0)
        table[a] = jnp.where(targets == iota, signs, 0.0).astype(jnp.bfloat16)
        return carry

    lax.fori_loop(0, rows, build, 0)

    for copy in gather_copies:
        copy.wait()
    widened[...] = gathered[...].astype(jnp.float32)

    def excite(g, carry):
        start = pl.multiple_of(g * ROWS, ROWS)
        source = source_ref[pl.ds(start, ROWS), :]
        sign = sign_b_ref[pl.ds(start, ROWS), :].astype(jnp.float32)
        block = source // LANES
        lane = source - block * LANES
        masks = [block == j for j in range(n_beta * cols // LANES)]
        for a in range(rows):
            value = None
            for j in range(n_beta * cols // LANES):
                row = widened[j, a : a + 1, :]
                picked = jnp.take_along_axis(
                    jnp.broadcast_to(row, (ROWS, LANES)), lane, axis=1, mode="promise_in_bounds"
                )
                value = picked if j == 0 else jnp.where(masks[j], picked, value)
            excited[pl.ds(start, ROWS), a * cols : (a + 1) * cols] = (value * sign).astype(
                jnp.bfloat16
            )
        return carry

    lax.fori_loop(0, pairs // ROWS, excite, 0)

    total[...] = jnp.zeros_like(total)

    def contract(p, carry):
        start = pl.multiple_of(p * 2 * cols, 2 * cols)
        mixed = jnp.dot(
            integrals_ref[...],
            excited[:, pl.ds(start, 2 * cols)],
            preferred_element_type=jnp.float32,
        ).astype(jnp.bfloat16)
        total[...] += jnp.dot(
            table[2 * p], mixed[:, :cols], preferred_element_type=jnp.float32
        ) + jnp.dot(table[2 * p + 1], mixed[:, cols:], preferred_element_type=jnp.float32)
        return carry

    lax.fori_loop(0, rows // 2, contract, 0)

    for i in range(n_alpha):
        outgoing[i] = total[i * rows : (i + 1) * rows, :].astype(jnp.bfloat16)
    sum_copies = []
    for d in range(1, n_alpha):
        to = lax.rem(ia + d, n_alpha)
        copy = pltpu.make_async_remote_copy(
            src_ref=outgoing.at[to],
            dst_ref=incoming.at[d - 1],
            send_sem=sum_send.at[d - 1],
            recv_sem=sum_recv.at[d - 1],
            device_id=(to, ib),
            device_id_type=MESH,
        )
        copy.start()
        sum_copies.append(copy)
    result = total[pl.ds(pl.multiple_of(ia * rows, rows), rows), :]
    for d in range(1, n_alpha):
        sum_copies[d - 1].wait()
        result = result + incoming[d - 1].astype(jnp.float32)
    out_ref[...] = result


def on_device(coeffs, integrals, source_beta, sign_beta, target_alpha, sign_alpha):
    n_alpha = lax.axis_size("alpha")
    n_beta = lax.axis_size("beta")
    rows, cols = coeffs.shape
    pairs = integrals.shape[0]
    all_alpha = rows * n_alpha
    vmem = pl.BlockSpec(memory_space=pltpu.VMEM)
    return pl.pallas_call(
        functools.partial(kernel, n_alpha, n_beta),
        out_shape=jax.ShapeDtypeStruct((rows, cols), jnp.float32),
        in_specs=[vmem] * 6,
        out_specs=vmem,
        scratch_shapes=[
            pltpu.VMEM((n_beta, rows, cols), jnp.bfloat16),
            pltpu.VMEM((n_beta, rows, cols), jnp.float32),
            pltpu.VMEM((pairs, rows * cols), jnp.bfloat16),
            pltpu.VMEM((rows, all_alpha, pairs), jnp.bfloat16),
            pltpu.VMEM((all_alpha, cols), jnp.float32),
            pltpu.VMEM((n_alpha, rows, cols), jnp.bfloat16),
            pltpu.VMEM((n_alpha - 1, rows, cols), jnp.bfloat16),
            pltpu.SemaphoreType.DMA((n_beta - 1,)),
            pltpu.SemaphoreType.DMA((n_beta - 1,)),
            pltpu.SemaphoreType.DMA((n_alpha - 1,)),
            pltpu.SemaphoreType.DMA((n_alpha - 1,)),
        ],
        compiler_params=pltpu.CompilerParams(
            collective_id=0, has_side_effects=True, vmem_limit_bytes=48 * 1024 * 1024
        ),
    )(coeffs, integrals, source_beta, sign_beta, target_alpha, sign_alpha)


def solution(mesh):
    placed = (
        P("alpha", "beta"),
        P(),
        P(None, "beta"),
        P(None, "beta"),
        P("alpha", None),
        P("alpha", None),
    )
    return jax.shard_map(
        on_device, mesh=mesh, in_specs=placed, out_specs=P("alpha", "beta"), check_vma=False
    )
```

```python
import functools

import jax
import jax.numpy as jnp
from jax import lax
from jax.experimental import pallas as pl
from jax.experimental.pallas import tpu as pltpu
from jax.sharding import PartitionSpec as P

MESH = pl.DeviceIdType.MESH
LANES = 128
ROWS = 16


def spread_gather(values, lanes):
    numbers = lax.GatherDimensionNumbers(
        offset_dims=(),
        collapsed_slice_dims=(1,),
        start_index_map=(1,),
        operand_batching_dims=(0,),
        start_indices_batching_dims=(0,),
    )
    return lax.gather(
        values,
        lanes[:, :, None],
        numbers,
        slice_sizes=(1, 1),
        mode=lax.GatherScatterMode.PROMISE_IN_BOUNDS,
    )


def kernel(
    n_alpha,
    n_beta,
    coeffs_hbm,
    integrals_hbm,
    source_hbm,
    sign_b_hbm,
    target_hbm,
    sign_a_hbm,
    out_ref,
    integrals_ref,
    source_ref,
    sign_b_ref,
    target_ref,
    sign_a_ref,
    gathered,
    spread,
    lane_ref,
    block_ref,
    sign_ref,
    excited_0,
    excited_1,
    mixed_0,
    mixed_1,
    table,
    total,
    outgoing,
    incoming,
    load_sem,
    gather_send,
    gather_recv,
    sum_send,
    sum_recv,
):
    rows, cols = coeffs_hbm.shape
    pairs = integrals_hbm.shape[0]
    all_alpha = rows * n_alpha
    blocks = n_beta * cols // LANES
    ia = lax.axis_index("alpha")
    ib = lax.axis_index("beta")

    barrier = pltpu.get_barrier_semaphore()
    for d in range(1, n_beta):
        pl.semaphore_signal(
            barrier, inc=1, device_id=(ia, lax.rem(ib + d, n_beta)), device_id_type=MESH
        )
    for d in range(1, n_alpha):
        pl.semaphore_signal(
            barrier, inc=1, device_id=(lax.rem(ia + d, n_alpha), ib), device_id_type=MESH
        )
    loads = [
        pltpu.make_async_copy(src, dst, load_sem.at[i])
        for i, (src, dst) in enumerate(
            (
                (target_hbm, target_ref),
                (sign_a_hbm, sign_a_ref),
                (source_hbm, source_ref),
                (sign_b_hbm, sign_b_ref),
                (coeffs_hbm, gathered.at[ib]),
                (integrals_hbm, integrals_ref),
            )
        )
    ]
    for load in loads:
        load.start()
    pl.semaphore_wait(barrier, n_beta + n_alpha - 2)

    gather_copies = []
    for d in range(1, n_beta):
        copy = pltpu.make_async_remote_copy(
            src_ref=coeffs_hbm,
            dst_ref=gathered.at[ib],
            send_sem=gather_send.at[d - 1],
            recv_sem=gather_recv.at[d - 1],
            device_id=(ia, lax.rem(ib + d, n_beta)),
            device_id_type=MESH,
        )
        copy.start()
        gather_copies.append(copy)

    loads[0].wait()
    loads[1].wait()
    iota = lax.broadcasted_iota(jnp.int32, (ROWS, pairs), 0)

    def build(a, carry):
        targets = (jnp.broadcast_to(target_ref[pl.ds(a, 1), :], (ROWS, pairs)) - iota).astype(
            jnp.int16
        )
        signs = (
            jnp.broadcast_to(sign_a_ref[pl.ds(a, 1), :], (ROWS, pairs))
            .astype(jnp.float32)
            .astype(jnp.bfloat16)
        )
        zero = jnp.zeros_like(signs)
        for i in range(all_alpha // ROWS):
            table[a, i * ROWS : (i + 1) * ROWS, :] = jnp.where(
                targets == jnp.int16(i * ROWS), signs, zero
            )
        return carry

    lax.fori_loop(0, rows, build, 0)

    loads[2].wait()
    loads[3].wait()
    source = source_ref[...]
    block = source // LANES
    lane_ref[...] = (source - block * LANES).astype(jnp.int16)
    block_ref[...] = block.astype(jnp.int16)
    sign_ref[...] = sign_b_ref[...].astype(jnp.float32).astype(jnp.bfloat16)
    total[...] = jnp.zeros_like(total)

    loads[4].wait()
    loads[5].wait()
    for copy in gather_copies:
        copy.wait()

    for j in range(blocks):
        for a in range(rows):
            spread[j, a] = jnp.broadcast_to(
                gathered[j, a : a + 1, :].astype(jnp.float32), (ROWS, LANES)
            ).astype(jnp.bfloat16)

    def excite(p, out):
        for g in range(pairs // ROWS):
            at = slice(g * ROWS, (g + 1) * ROWS)
            lane = lane_ref[at, :]
            block = block_ref[at, :]
            sign = sign_ref[at, :]
            masks = [block == jnp.int16(j) for j in range(blocks)]
            for i in range(2):
                value = None
                for j in range(blocks):
                    picked = spread_gather(spread[j, 2 * p + i], lane)
                    value = picked if j == 0 else jnp.where(masks[j], picked, value)
                out[at, i * cols : (i + 1) * cols] = value * sign

    def contract(src, out):
        out[...] = jnp.dot(
            integrals_ref[...], src[...], preferred_element_type=jnp.float32
        ).astype(jnp.bfloat16)

    def scatter(p, src):
        total[...] += jnp.dot(
            table[2 * p], src[:, :cols], preferred_element_type=jnp.float32
        ) + jnp.dot(table[2 * p + 1], src[:, cols:], preferred_element_type=jnp.float32)

    excite(0, excited_0)
    contract(excited_0, mixed_0)
    excite(1, excited_1)

    def step(s, carry):
        p = 2 * s
        excite(p + 2, excited_0)
        contract(excited_1, mixed_1)
        scatter(p, mixed_0)
        excite(p + 3, excited_1)
        contract(excited_0, mixed_0)
        scatter(p + 1, mixed_1)
        return carry

    lax.fori_loop(0, rows // 4 - 1, step, 0)
    contract(excited_1, mixed_1)
    scatter(rows // 2 - 2, mixed_0)
    scatter(rows // 2 - 1, mixed_1)

    for i in range(n_alpha):
        outgoing[i] = total[i * rows : (i + 1) * rows, :].astype(jnp.bfloat16)
    sum_copies = []
    for d in range(1, n_alpha):
        to = lax.rem(ia + d, n_alpha)
        copy = pltpu.make_async_remote_copy(
            src_ref=outgoing.at[to],
            dst_ref=incoming.at[d - 1],
            send_sem=sum_send.at[d - 1],
            recv_sem=sum_recv.at[d - 1],
            device_id=(to, ib),
            device_id_type=MESH,
        )
        copy.start()
        sum_copies.append(copy)
    result = total[pl.ds(pl.multiple_of(ia * rows, rows), rows), :]
    for d in range(1, n_alpha):
        sum_copies[d - 1].wait()
        result = result + incoming[d - 1].astype(jnp.float32)
    out_ref[...] = result


def on_device(coeffs, integrals, source_beta, sign_beta, target_alpha, sign_alpha):
    n_alpha = lax.axis_size("alpha")
    n_beta = lax.axis_size("beta")
    rows, cols = coeffs.shape
    pairs = integrals.shape[0]
    all_alpha = rows * n_alpha
    blocks = n_beta * cols // LANES
    return pl.pallas_call(
        functools.partial(kernel, n_alpha, n_beta),
        out_shape=jax.ShapeDtypeStruct((rows, cols), jnp.float32),
        in_specs=[pl.BlockSpec(memory_space=pl.ANY)] * 6,
        out_specs=pl.BlockSpec(memory_space=pltpu.VMEM),
        scratch_shapes=[
            pltpu.VMEM((pairs, pairs), jnp.bfloat16),
            pltpu.VMEM((pairs, cols), jnp.int32),
            pltpu.VMEM((pairs, cols), jnp.int32),
            pltpu.VMEM((rows, pairs), jnp.int32),
            pltpu.VMEM((rows, pairs), jnp.int32),
            pltpu.VMEM((n_beta, rows, cols), jnp.bfloat16),
            pltpu.VMEM((blocks, rows, ROWS, LANES), jnp.bfloat16),
            pltpu.VMEM((pairs, cols), jnp.int16),
            pltpu.VMEM((pairs, cols), jnp.int16),
            pltpu.VMEM((pairs, cols), jnp.bfloat16),
            pltpu.VMEM((pairs, 2 * cols), jnp.bfloat16),
            pltpu.VMEM((pairs, 2 * cols), jnp.bfloat16),
            pltpu.VMEM((pairs, 2 * cols), jnp.bfloat16),
            pltpu.VMEM((pairs, 2 * cols), jnp.bfloat16),
            pltpu.VMEM((rows, all_alpha, pairs), jnp.bfloat16),
            pltpu.VMEM((all_alpha, cols), jnp.float32),
            pltpu.VMEM((n_alpha, rows, cols), jnp.bfloat16),
            pltpu.VMEM((n_alpha - 1, rows, cols), jnp.bfloat16),
            pltpu.SemaphoreType.DMA((6,)),
            pltpu.SemaphoreType.DMA((n_beta - 1,)),
            pltpu.SemaphoreType.DMA((n_beta - 1,)),
            pltpu.SemaphoreType.DMA((n_alpha - 1,)),
            pltpu.SemaphoreType.DMA((n_alpha - 1,)),
        ],
        compiler_params=pltpu.CompilerParams(
            collective_id=0, has_side_effects=True, vmem_limit_bytes=56 * 1024 * 1024
        ),
    )(coeffs, integrals, source_beta, sign_beta, target_alpha, sign_alpha)


def solution(mesh):
    placed = (
        P("alpha", "beta"),
        P(),
        P(None, "beta"),
        P(None, "beta"),
        P("alpha", None),
        P("alpha", None),
    )
    return jax.shard_map(
        on_device, mesh=mesh, in_specs=placed, out_specs=P("alpha", "beta"), check_vma=False
    )
```

```python
import functools

import jax
import jax.numpy as jnp
from jax import lax
from jax.experimental import pallas as pl
from jax.experimental.pallas import tpu as pltpu
from jax.sharding import PartitionSpec as P

MESH = pl.DeviceIdType.MESH
LANES = 128
ROWS = 16


def spread_gather(values, lanes):
    numbers = lax.GatherDimensionNumbers(
        offset_dims=(),
        collapsed_slice_dims=(1,),
        start_index_map=(1,),
        operand_batching_dims=(0,),
        start_indices_batching_dims=(0,),
    )
    return lax.gather(
        values,
        lanes[:, :, None],
        numbers,
        slice_sizes=(1, 1),
        mode=lax.GatherScatterMode.PROMISE_IN_BOUNDS,
    )


def kernel(
    n_alpha,
    n_beta,
    coeffs_hbm,
    integrals_hbm,
    source_hbm,
    sign_b_hbm,
    target_hbm,
    sign_a_hbm,
    out_ref,
    integrals_ref,
    source_ref,
    sign_b_ref,
    target_ref,
    sign_a_ref,
    gathered,
    spread,
    lane_ref,
    slot_ref,
    sign_ref,
    base,
    excited_0,
    excited_1,
    mixed_0,
    mixed_1,
    table_0,
    table_1,
    total,
    outgoing,
    incoming,
    load_sem,
    gather_send,
    gather_recv,
    sum_send,
    sum_recv,
):
    rows, cols = coeffs_hbm.shape
    pairs = integrals_hbm.shape[0]
    all_alpha = rows * n_alpha
    ia = lax.axis_index("alpha")
    ib = lax.axis_index("beta")

    barrier = pltpu.get_barrier_semaphore()
    for d in range(1, n_beta):
        pl.semaphore_signal(
            barrier, inc=1, device_id=(ia, lax.rem(ib + d, n_beta)), device_id_type=MESH
        )
    for d in range(1, n_alpha):
        pl.semaphore_signal(
            barrier, inc=1, device_id=(lax.rem(ia + d, n_alpha), ib), device_id_type=MESH
        )
    loads = [
        pltpu.make_async_copy(src, dst, load_sem.at[i])
        for i, (src, dst) in enumerate(
            (
                (coeffs_hbm, gathered.at[0]),
                (source_hbm, source_ref),
                (sign_b_hbm, sign_b_ref),
                (target_hbm, target_ref),
                (sign_a_hbm, sign_a_ref),
                (integrals_hbm, integrals_ref),
            )
        )
    ]
    for load in loads:
        load.start()
    pl.semaphore_wait(barrier, n_beta + n_alpha - 2)

    gather_copies = []
    for d in range(1, n_beta):
        copy = pltpu.make_async_remote_copy(
            src_ref=coeffs_hbm,
            dst_ref=gathered.at[d],
            send_sem=gather_send.at[d - 1],
            recv_sem=gather_recv.at[d - 1],
            device_id=(ia, lax.rem(ib + d, n_beta)),
            device_id_type=MESH,
        )
        copy.start()
        gather_copies.append(copy)

    loads[0].wait()
    loads[1].wait()
    source = source_ref[...]
    block = source // LANES
    lane_ref[...] = (source - block * LANES).astype(jnp.int16)
    slot = ib - block
    slot_ref[...] = jnp.where(slot < 0, slot + n_beta, slot).astype(jnp.int16)

    def spread_rows(d):
        for a in range(rows):
            spread[d, a] = jnp.broadcast_to(
                gathered[d, a : a + 1, :].astype(jnp.float32), (ROWS, LANES)
            ).astype(jnp.bfloat16)

    spread_rows(0)

    def excite_own(g, carry):
        at = pl.ds(pl.multiple_of(g * ROWS, ROWS), ROWS)
        lane = lane_ref[at, :]
        for a in range(rows):
            base[a // 2, at, (a % 2) * cols : (a % 2 + 1) * cols] = spread_gather(
                spread[0, a], lane
            )
        return carry

    lax.fori_loop(0, pairs // ROWS, excite_own, 0)

    loads[2].wait()
    sign_ref[...] = sign_b_ref[...].astype(jnp.float32).astype(jnp.bfloat16)
    total[...] = jnp.zeros_like(total)
    for load in loads[3:]:
        load.wait()
    for copy in gather_copies:
        copy.wait()
    for d in range(1, n_beta):
        spread_rows(d)

    def excite(p, out):
        for g in range(pairs // ROWS):
            at = slice(g * ROWS, (g + 1) * ROWS)
            lane = lane_ref[at, :]
            slot = slot_ref[at, :]
            sign = sign_ref[at, :]
            masks = [slot == jnp.int16(d) for d in range(n_beta)]
            for i in range(2):
                value = base[p, at, i * cols : (i + 1) * cols]
                for d in range(1, n_beta):
                    value = jnp.where(masks[d], spread_gather(spread[d, 2 * p + i], lane), value)
                out[at, i * cols : (i + 1) * cols] = value * sign

    def contract(src, out):
        out[...] = jnp.dot(
            integrals_ref[...], src[...], preferred_element_type=jnp.float32
        ).astype(jnp.bfloat16)

    iota = lax.broadcasted_iota(jnp.int32, (ROWS, pairs), 0)

    def build(p, out):
        for i in range(2):
            row = pl.ds(2 * p + i, 1)
            targets = (jnp.broadcast_to(target_ref[row, :], (ROWS, pairs)) - iota).astype(jnp.int16)
            signs = (
                jnp.broadcast_to(sign_a_ref[row, :], (ROWS, pairs))
                .astype(jnp.float32)
                .astype(jnp.bfloat16)
            )
            zero = jnp.zeros_like(signs)
            for k in range(all_alpha // ROWS):
                out[i, k * ROWS : (k + 1) * ROWS, :] = jnp.where(
                    targets == jnp.int16(k * ROWS), signs, zero
                )

    def scatter(table, src):
        total[...] += jnp.dot(
            table[0], src[:, :cols], preferred_element_type=jnp.float32
        ) + jnp.dot(table[1], src[:, cols:], preferred_element_type=jnp.float32)

    excite(0, excited_0)
    contract(excited_0, mixed_0)
    build(0, table_0)
    excite(1, excited_1)

    def step(s, carry):
        p = 2 * s
        excite(p + 2, excited_0)
        contract(excited_1, mixed_1)
        build(p + 1, table_1)
        scatter(table_0, mixed_0)
        excite(p + 3, excited_1)
        contract(excited_0, mixed_0)
        build(p + 2, table_0)
        scatter(table_1, mixed_1)
        return carry

    lax.fori_loop(0, rows // 4 - 1, step, 0)
    contract(excited_1, mixed_1)
    build(rows // 2 - 1, table_1)
    scatter(table_0, mixed_0)
    scatter(table_1, mixed_1)

    for i in range(n_alpha):
        outgoing[i] = total[i * rows : (i + 1) * rows, :].astype(jnp.bfloat16)
    sum_copies = []
    for d in range(1, n_alpha):
        to = lax.rem(ia + d, n_alpha)
        copy = pltpu.make_async_remote_copy(
            src_ref=outgoing.at[to],
            dst_ref=incoming.at[d - 1],
            send_sem=sum_send.at[d - 1],
            recv_sem=sum_recv.at[d - 1],
            device_id=(to, ib),
            device_id_type=MESH,
        )
        copy.start()
        sum_copies.append(copy)
    result = total[pl.ds(pl.multiple_of(ia * rows, rows), rows), :]
    for d in range(1, n_alpha):
        sum_copies[d - 1].wait()
        result = result + incoming[d - 1].astype(jnp.float32)
    out_ref[...] = result


def on_device(coeffs, integrals, source_beta, sign_beta, target_alpha, sign_alpha):
    n_alpha = lax.axis_size("alpha")
    n_beta = lax.axis_size("beta")
    rows, cols = coeffs.shape
    pairs = integrals.shape[0]
    all_alpha = rows * n_alpha
    operands = [
        pltpu.with_memory_space_constraint(array, pltpu.HBM)
        for array in (coeffs, integrals, source_beta, sign_beta, target_alpha, sign_alpha)
    ]
    return pl.pallas_call(
        functools.partial(kernel, n_alpha, n_beta),
        out_shape=jax.ShapeDtypeStruct((rows, cols), jnp.float32),
        in_specs=[pl.BlockSpec(memory_space=pltpu.HBM)] * 6,
        out_specs=pl.BlockSpec(memory_space=pltpu.VMEM),
        scratch_shapes=[
            pltpu.VMEM((pairs, pairs), jnp.bfloat16),
            pltpu.VMEM((pairs, cols), jnp.int32),
            pltpu.VMEM((pairs, cols), jnp.int32),
            pltpu.VMEM((rows, pairs), jnp.int32),
            pltpu.VMEM((rows, pairs), jnp.int32),
            pltpu.VMEM((n_beta, rows, cols), jnp.bfloat16),
            pltpu.VMEM((n_beta, rows, ROWS, LANES), jnp.bfloat16),
            pltpu.VMEM((pairs, cols), jnp.int16),
            pltpu.VMEM((pairs, cols), jnp.int16),
            pltpu.VMEM((pairs, cols), jnp.bfloat16),
            pltpu.VMEM((rows // 2, pairs, 2 * cols), jnp.bfloat16),
            pltpu.VMEM((pairs, 2 * cols), jnp.bfloat16),
            pltpu.VMEM((pairs, 2 * cols), jnp.bfloat16),
            pltpu.VMEM((pairs, 2 * cols), jnp.bfloat16),
            pltpu.VMEM((pairs, 2 * cols), jnp.bfloat16),
            pltpu.VMEM((2, all_alpha, pairs), jnp.bfloat16),
            pltpu.VMEM((2, all_alpha, pairs), jnp.bfloat16),
            pltpu.VMEM((all_alpha, cols), jnp.float32),
            pltpu.VMEM((n_alpha, rows, cols), jnp.bfloat16),
            pltpu.VMEM((n_alpha - 1, rows, cols), jnp.bfloat16),
            pltpu.SemaphoreType.DMA((6,)),
            pltpu.SemaphoreType.DMA((n_beta - 1,)),
            pltpu.SemaphoreType.DMA((n_beta - 1,)),
            pltpu.SemaphoreType.DMA((n_alpha - 1,)),
            pltpu.SemaphoreType.DMA((n_alpha - 1,)),
        ],
        compiler_params=pltpu.CompilerParams(
            collective_id=0, has_side_effects=True, vmem_limit_bytes=32 * 1024 * 1024
        ),
    )(*operands)


def solution(mesh):
    placed = (
        P("alpha", "beta"),
        P(),
        P(None, "beta"),
        P(None, "beta"),
        P("alpha", None),
        P("alpha", None),
    )
    return jax.shard_map(
        on_device, mesh=mesh, in_specs=placed, out_specs=P("alpha", "beta"), check_vma=False
    )
```

```python
import functools

import jax
import jax.numpy as jnp
from jax import lax
from jax.experimental import pallas as pl
from jax.experimental.pallas import tpu as pltpu
from jax.sharding import PartitionSpec as P

MESH = pl.DeviceIdType.MESH
LANES = 128
ROWS = 16


def spread_gather(values, lanes):
    numbers = lax.GatherDimensionNumbers(
        offset_dims=(),
        collapsed_slice_dims=(1,),
        start_index_map=(1,),
        operand_batching_dims=(0,),
        start_indices_batching_dims=(0,),
    )
    return lax.gather(
        values,
        lanes[:, :, None],
        numbers,
        slice_sizes=(1, 1),
        mode=lax.GatherScatterMode.PROMISE_IN_BOUNDS,
    )


def kernel(
    n_alpha,
    n_beta,
    coeffs_hbm,
    integrals_hbm,
    source_hbm,
    sign_b_hbm,
    target_hbm,
    sign_a_hbm,
    out_ref,
    integrals_ref,
    source_ref,
    sign_b_ref,
    target_ref,
    sign_a_ref,
    gathered,
    spread,
    lane_ref,
    slot_ref,
    sign_ref,
    base,
    excited_0,
    excited_1,
    mixed_0,
    mixed_1,
    table_0,
    table_1,
    total,
    outgoing,
    incoming,
    load_sem,
    gather_send,
    gather_recv,
    sum_send,
    sum_recv,
):
    rows, cols = coeffs_hbm.shape
    pairs = integrals_hbm.shape[0]
    all_alpha = rows * n_alpha
    ia = lax.axis_index("alpha")
    ib = lax.axis_index("beta")

    barrier = pltpu.get_barrier_semaphore()
    for d in range(1, n_beta):
        pl.semaphore_signal(
            barrier, inc=1, device_id=(ia, lax.rem(ib + d, n_beta)), device_id_type=MESH
        )
    for d in range(1, n_alpha):
        pl.semaphore_signal(
            barrier, inc=1, device_id=(lax.rem(ia + d, n_alpha), ib), device_id_type=MESH
        )
    loads = [
        pltpu.make_async_copy(src, dst, load_sem.at[i])
        for i, (src, dst) in enumerate(
            (
                (coeffs_hbm, gathered.at[0]),
                (source_hbm, source_ref),
                (sign_b_hbm, sign_b_ref),
                (target_hbm, target_ref),
                (sign_a_hbm, sign_a_ref),
                (integrals_hbm, integrals_ref),
            )
        )
    ]
    for load in loads:
        load.start()
    pl.semaphore_wait(barrier, n_beta + n_alpha - 2)

    gather_copies = []
    for d in range(1, n_beta):
        copy = pltpu.make_async_remote_copy(
            src_ref=coeffs_hbm,
            dst_ref=gathered.at[d],
            send_sem=gather_send.at[d - 1],
            recv_sem=gather_recv.at[d - 1],
            device_id=(ia, lax.rem(ib + d, n_beta)),
            device_id_type=MESH,
        )
        copy.start()
        gather_copies.append(copy)

    loads[0].wait()
    loads[1].wait()
    source = source_ref[...]
    block = source // LANES
    lane_ref[...] = (source - block * LANES).astype(jnp.int16)
    slot = ib - block
    slot_ref[...] = jnp.where(slot < 0, slot + n_beta, slot).astype(jnp.int16)

    def spread_rows(d):
        for a in range(rows):
            spread[d, a] = jnp.broadcast_to(
                gathered[d, a : a + 1, :].astype(jnp.float32), (ROWS, LANES)
            ).astype(jnp.bfloat16)

    spread_rows(0)

    def excite_own(g, carry):
        at = pl.ds(pl.multiple_of(g * ROWS, ROWS), ROWS)
        lane = lane_ref[at, :]
        for a in range(rows):
            base[a // 2, at, (a % 2) * cols : (a % 2 + 1) * cols] = spread_gather(
                spread[0, a], lane
            )
        return carry

    lax.fori_loop(0, pairs // ROWS, excite_own, 0)

    loads[2].wait()
    sign_ref[...] = sign_b_ref[...].astype(jnp.float32).astype(jnp.bfloat16)
    total[...] = jnp.zeros_like(total)
    for load in loads[3:]:
        load.wait()
    for copy in gather_copies:
        copy.wait()
    for d in range(1, n_beta):
        spread_rows(d)

    groups = pairs // ROWS

    def excite(p, out, first=0, last=groups):
        for g in range(first, last):
            at = slice(g * ROWS, (g + 1) * ROWS)
            lane = lane_ref[at, :]
            slot = slot_ref[at, :]
            sign = sign_ref[at, :]
            masks = [slot == jnp.int16(d) for d in range(n_beta)]
            for i in range(2):
                value = base[p, at, i * cols : (i + 1) * cols]
                for d in range(1, n_beta):
                    value = jnp.where(masks[d], spread_gather(spread[d, 2 * p + i], lane), value)
                out[at, i * cols : (i + 1) * cols] = value * sign

    def contract(src, out):
        out[...] = jnp.dot(
            integrals_ref[...], src[...], preferred_element_type=jnp.float32
        ).astype(jnp.bfloat16)

    iota = lax.broadcasted_iota(jnp.int32, (ROWS, pairs), 0)

    def build(p, out, i):
        row = pl.ds(2 * p + i, 1)
        targets = (jnp.broadcast_to(target_ref[row, :], (ROWS, pairs)) - iota).astype(jnp.int16)
        signs = (
            jnp.broadcast_to(sign_a_ref[row, :], (ROWS, pairs))
            .astype(jnp.float32)
            .astype(jnp.bfloat16)
        )
        zero = jnp.zeros_like(signs)
        for k in range(all_alpha // ROWS):
            out[i, k * ROWS : (k + 1) * ROWS, :] = jnp.where(
                targets == jnp.int16(k * ROWS), signs, zero
            )

    def scatter(table, src, i):
        total[...] += jnp.dot(
            table[i], src[:, i * cols : (i + 1) * cols], preferred_element_type=jnp.float32
        )

    third = -(-groups // 3)

    def stages(p, here, there, mixed, mixed_next, table, table_next):
        contract(there, mixed_next)
        excite(p + 2, here, 0, third)
        build(p + 1, table_next, 0)
        scatter(table, mixed, 0)
        excite(p + 2, here, third, 2 * third)
        build(p + 1, table_next, 1)
        scatter(table, mixed, 1)
        excite(p + 2, here, 2 * third, groups)

    excite(0, excited_0)
    contract(excited_0, mixed_0)
    build(0, table_0, 0)
    build(0, table_0, 1)
    excite(1, excited_1)

    def step(s, carry):
        p = 2 * s
        stages(p, excited_0, excited_1, mixed_0, mixed_1, table_0, table_1)
        stages(p + 1, excited_1, excited_0, mixed_1, mixed_0, table_1, table_0)
        return carry

    lax.fori_loop(0, rows // 4 - 1, step, 0)
    contract(excited_1, mixed_1)
    build(rows // 2 - 1, table_1, 0)
    build(rows // 2 - 1, table_1, 1)
    for table, mixed in ((table_0, mixed_0), (table_1, mixed_1)):
        scatter(table, mixed, 0)
        scatter(table, mixed, 1)

    for i in range(n_alpha):
        outgoing[i] = total[i * rows : (i + 1) * rows, :].astype(jnp.bfloat16)
    sum_copies = []
    for d in range(1, n_alpha):
        to = lax.rem(ia + d, n_alpha)
        copy = pltpu.make_async_remote_copy(
            src_ref=outgoing.at[to],
            dst_ref=incoming.at[d - 1],
            send_sem=sum_send.at[d - 1],
            recv_sem=sum_recv.at[d - 1],
            device_id=(to, ib),
            device_id_type=MESH,
        )
        copy.start()
        sum_copies.append(copy)
    result = total[pl.ds(pl.multiple_of(ia * rows, rows), rows), :]
    for d in range(1, n_alpha):
        sum_copies[d - 1].wait()
        result = result + incoming[d - 1].astype(jnp.float32)
    out_ref[...] = result


def on_device(coeffs, integrals, source_beta, sign_beta, target_alpha, sign_alpha):
    n_alpha = lax.axis_size("alpha")
    n_beta = lax.axis_size("beta")
    rows, cols = coeffs.shape
    pairs = integrals.shape[0]
    all_alpha = rows * n_alpha
    operands = [
        pltpu.with_memory_space_constraint(array, pltpu.HBM)
        for array in (coeffs, integrals, source_beta, sign_beta, target_alpha, sign_alpha)
    ]
    return pl.pallas_call(
        functools.partial(kernel, n_alpha, n_beta),
        out_shape=jax.ShapeDtypeStruct((rows, cols), jnp.float32),
        in_specs=[pl.BlockSpec(memory_space=pltpu.HBM)] * 6,
        out_specs=pl.BlockSpec(memory_space=pltpu.VMEM),
        scratch_shapes=[
            pltpu.VMEM((pairs, pairs), jnp.bfloat16),
            pltpu.VMEM((pairs, cols), jnp.int32),
            pltpu.VMEM((pairs, cols), jnp.int32),
            pltpu.VMEM((rows, pairs), jnp.int32),
            pltpu.VMEM((rows, pairs), jnp.int32),
            pltpu.VMEM((n_beta, rows, cols), jnp.bfloat16),
            pltpu.VMEM((n_beta, rows, ROWS, LANES), jnp.bfloat16),
            pltpu.VMEM((pairs, cols), jnp.int16),
            pltpu.VMEM((pairs, cols), jnp.int16),
            pltpu.VMEM((pairs, cols), jnp.bfloat16),
            pltpu.VMEM((rows // 2, pairs, 2 * cols), jnp.bfloat16),
            pltpu.VMEM((pairs, 2 * cols), jnp.bfloat16),
            pltpu.VMEM((pairs, 2 * cols), jnp.bfloat16),
            pltpu.VMEM((pairs, 2 * cols), jnp.bfloat16),
            pltpu.VMEM((pairs, 2 * cols), jnp.bfloat16),
            pltpu.VMEM((2, all_alpha, pairs), jnp.bfloat16),
            pltpu.VMEM((2, all_alpha, pairs), jnp.bfloat16),
            pltpu.VMEM((all_alpha, cols), jnp.float32),
            pltpu.VMEM((n_alpha, rows, cols), jnp.bfloat16),
            pltpu.VMEM((n_alpha - 1, rows, cols), jnp.bfloat16),
            pltpu.SemaphoreType.DMA((6,)),
            pltpu.SemaphoreType.DMA((n_beta - 1,)),
            pltpu.SemaphoreType.DMA((n_beta - 1,)),
            pltpu.SemaphoreType.DMA((n_alpha - 1,)),
            pltpu.SemaphoreType.DMA((n_alpha - 1,)),
        ],
        compiler_params=pltpu.CompilerParams(
            collective_id=0, has_side_effects=True, vmem_limit_bytes=32 * 1024 * 1024
        ),
    )(*operands)


def solution(mesh):
    placed = (
        P("alpha", "beta"),
        P(),
        P(None, "beta"),
        P(None, "beta"),
        P("alpha", None),
        P("alpha", None),
    )
    return jax.shard_map(
        on_device, mesh=mesh, in_specs=placed, out_specs=P("alpha", "beta"), check_vma=False
    )
```

```python
import functools

import jax
import jax.numpy as jnp
from jax import lax
from jax.experimental import pallas as pl
from jax.experimental.pallas import tpu as pltpu
from jax.sharding import PartitionSpec as P

MESH = pl.DeviceIdType.MESH
LANES = 128
ROWS = 16
WIDE = 4


def spread_gather(values, lanes):
    numbers = lax.GatherDimensionNumbers(
        offset_dims=(),
        collapsed_slice_dims=(1,),
        start_index_map=(1,),
        operand_batching_dims=(0,),
        start_indices_batching_dims=(0,),
    )
    return lax.gather(
        values,
        lanes[:, :, None],
        numbers,
        slice_sizes=(1, 1),
        mode=lax.GatherScatterMode.PROMISE_IN_BOUNDS,
    )


def kernel(
    n_alpha,
    n_beta,
    coeffs_hbm,
    integrals_hbm,
    source_hbm,
    sign_b_hbm,
    target_hbm,
    sign_a_hbm,
    out_ref,
    integrals_ref,
    source_ref,
    sign_b_ref,
    target_ref,
    sign_a_ref,
    target_flat,
    sign_a_flat,
    gathered,
    spread,
    lane_ref,
    slot_ref,
    sign_ref,
    base,
    excited_0,
    excited_1,
    mixed_0,
    mixed_1,
    table_0,
    table_1,
    total,
    outgoing,
    incoming,
    load_sem,
    gather_send,
    gather_recv,
    sum_send,
    sum_recv,
):
    rows, cols = coeffs_hbm.shape
    pairs = integrals_hbm.shape[0]
    all_alpha = rows * n_alpha
    ia = lax.axis_index("alpha")
    ib = lax.axis_index("beta")

    sets = rows // WIDE

    barrier = pltpu.get_barrier_semaphore()
    for d in range(1, n_beta):
        pl.semaphore_signal(
            barrier, inc=1, device_id=(ia, lax.rem(ib + d, n_beta)), device_id_type=MESH
        )
    for d in range(1, n_alpha):
        pl.semaphore_signal(
            barrier, inc=1, device_id=(lax.rem(ia + d, n_alpha), ib), device_id_type=MESH
        )
    loads = [
        pltpu.make_async_copy(src, dst, load_sem.at[i])
        for i, (src, dst) in enumerate(
            (
                (coeffs_hbm, gathered.at[0]),
                (source_hbm, source_ref),
                (sign_b_hbm, sign_b_ref),
                (target_hbm, target_ref),
                (sign_a_hbm, sign_a_ref),
                (integrals_hbm, integrals_ref),
            )
        )
    ]
    for load in loads:
        load.start()
    pl.semaphore_wait(barrier, n_beta + n_alpha - 2)

    gather_copies = []
    for d in range(1, n_beta):
        copy = pltpu.make_async_remote_copy(
            src_ref=coeffs_hbm,
            dst_ref=gathered.at[d],
            send_sem=gather_send.at[d - 1],
            recv_sem=gather_recv.at[d - 1],
            device_id=(ia, lax.rem(ib + d, n_beta)),
            device_id_type=MESH,
        )
        copy.start()
        gather_copies.append(copy)

    loads[0].wait()
    loads[1].wait()
    source = source_ref[...]
    block = source // LANES
    lane_ref[...] = (source - block * LANES).astype(jnp.int16)
    slot = ib - block
    slot_ref[...] = jnp.where(slot < 0, slot + n_beta, slot).astype(jnp.int16)

    def spread_rows(d):
        for a in range(rows):
            spread[d, a] = jnp.broadcast_to(
                gathered[d, a : a + 1, :].astype(jnp.float32), (ROWS, LANES)
            ).astype(jnp.bfloat16)

    spread_rows(0)

    def excite_own(g, carry):
        at = pl.ds(pl.multiple_of(g * ROWS, ROWS), ROWS)
        lane = lane_ref[at, :]
        for a in range(rows):
            base[a % sets, at, (a // sets) * cols : (a // sets + 1) * cols] = spread_gather(
                spread[0, a], lane
            )
        return carry

    lax.fori_loop(0, pairs // ROWS, excite_own, 0)

    loads[2].wait()
    sign_ref[...] = sign_b_ref[...].astype(jnp.float32).astype(jnp.bfloat16)
    total[...] = jnp.zeros_like(total)
    for load in loads[3:]:
        load.wait()
    for src, dst in ((target_ref, target_flat), (sign_a_ref, sign_a_flat)):
        dst[...] = jnp.concatenate(
            [src[i * sets : (i + 1) * sets, :] for i in range(WIDE)], axis=1
        )
    for copy in gather_copies:
        copy.wait()
    for d in range(1, n_beta):
        spread_rows(d)

    groups = pairs // ROWS

    def excite_group(p, out, at):
        lane = lane_ref[at, :]
        slot = slot_ref[at, :]
        sign = sign_ref[at, :]
        masks = [slot == jnp.int16(d) for d in range(n_beta)]
        for i in range(WIDE):
            value = base[p, at, i * cols : (i + 1) * cols]
            for d in range(1, n_beta):
                value = jnp.where(masks[d], spread_gather(spread[d, i * sets + p], lane), value)
            out[at, i * cols : (i + 1) * cols] = value * sign

    def excite(p, out, first, last):
        for g in range(first, last):
            excite_group(p, out, slice(g * ROWS, (g + 1) * ROWS))

    def excite_looped(p, out):
        def one(g, carry):
            excite_group(p, out, pl.ds(pl.multiple_of(g * ROWS, ROWS), ROWS))
            return carry

        lax.fori_loop(0, groups, one, 0)

    def contract(src, out):
        mixed = jnp.dot(
            integrals_ref[...], src[...], preferred_element_type=jnp.float32
        ).astype(jnp.bfloat16)
        for i in range(WIDE):
            out[i * pairs : (i + 1) * pairs, :] = mixed[:, i * cols : (i + 1) * cols]

    iota = lax.broadcasted_iota(jnp.int32, (ROWS, WIDE * pairs), 0)

    def build(p, out):
        row = pl.ds(p, 1)
        shape = (ROWS, WIDE * pairs)
        targets = (jnp.broadcast_to(target_flat[row, :], shape) - iota).astype(jnp.int16)
        signs = (
            jnp.broadcast_to(sign_a_flat[row, :], shape).astype(jnp.float32).astype(jnp.bfloat16)
        )
        zero = jnp.zeros_like(signs)
        for k in range(all_alpha // ROWS):
            out[k * ROWS : (k + 1) * ROWS, :] = jnp.where(
                targets == jnp.int16(k * ROWS), signs, zero
            )

    def scatter(table, mixed):
        total[...] += jnp.dot(table[...], mixed[...], preferred_element_type=jnp.float32)

    def stages(p, here, there, mixed, mixed_next, table, table_next):
        contract(there, mixed_next)
        excite(p + 2, here, 0, groups // 2)
        build(p + 1, table_next)
        scatter(table, mixed)
        excite(p + 2, here, groups // 2, groups)

    excite_looped(0, excited_0)
    contract(excited_0, mixed_0)
    build(0, table_0)
    excite_looped(1, excited_1)

    def step(s, carry):
        p = 2 * s
        stages(p, excited_0, excited_1, mixed_0, mixed_1, table_0, table_1)
        stages(p + 1, excited_1, excited_0, mixed_1, mixed_0, table_1, table_0)
        return carry

    lax.fori_loop(0, sets // 2 - 1, step, 0)
    contract(excited_1, mixed_1)
    build(sets - 1, table_1)
    scatter(table_0, mixed_0)
    scatter(table_1, mixed_1)

    for i in range(n_alpha):
        outgoing[i] = total[i * rows : (i + 1) * rows, :].astype(jnp.bfloat16)
    sum_copies = []
    for d in range(1, n_alpha):
        to = lax.rem(ia + d, n_alpha)
        copy = pltpu.make_async_remote_copy(
            src_ref=outgoing.at[to],
            dst_ref=incoming.at[d - 1],
            send_sem=sum_send.at[d - 1],
            recv_sem=sum_recv.at[d - 1],
            device_id=(to, ib),
            device_id_type=MESH,
        )
        copy.start()
        sum_copies.append(copy)
    result = total[pl.ds(pl.multiple_of(ia * rows, rows), rows), :]
    for d in range(1, n_alpha):
        sum_copies[d - 1].wait()
        result = result + incoming[d - 1].astype(jnp.float32)
    out_ref[...] = result


def on_device(coeffs, integrals, source_beta, sign_beta, target_alpha, sign_alpha):
    n_alpha = lax.axis_size("alpha")
    n_beta = lax.axis_size("beta")
    rows, cols = coeffs.shape
    pairs = integrals.shape[0]
    all_alpha = rows * n_alpha
    operands = [
        pltpu.with_memory_space_constraint(array, pltpu.HBM)
        for array in (coeffs, integrals, source_beta, sign_beta, target_alpha, sign_alpha)
    ]
    return pl.pallas_call(
        functools.partial(kernel, n_alpha, n_beta),
        out_shape=jax.ShapeDtypeStruct((rows, cols), jnp.float32),
        in_specs=[pl.BlockSpec(memory_space=pltpu.HBM)] * 6,
        out_specs=pl.BlockSpec(memory_space=pltpu.VMEM),
        scratch_shapes=[
            pltpu.VMEM((pairs, pairs), jnp.bfloat16),
            pltpu.VMEM((pairs, cols), jnp.int32),
            pltpu.VMEM((pairs, cols), jnp.int32),
            pltpu.VMEM((rows, pairs), jnp.int32),
            pltpu.VMEM((rows, pairs), jnp.int32),
            pltpu.VMEM((rows // WIDE, WIDE * pairs), jnp.int32),
            pltpu.VMEM((rows // WIDE, WIDE * pairs), jnp.int32),
            pltpu.VMEM((n_beta, rows, cols), jnp.bfloat16),
            pltpu.VMEM((n_beta, rows, ROWS, LANES), jnp.bfloat16),
            pltpu.VMEM((pairs, cols), jnp.int16),
            pltpu.VMEM((pairs, cols), jnp.int16),
            pltpu.VMEM((pairs, cols), jnp.bfloat16),
            pltpu.VMEM((rows // WIDE, pairs, WIDE * cols), jnp.bfloat16),
            pltpu.VMEM((pairs, WIDE * cols), jnp.bfloat16),
            pltpu.VMEM((pairs, WIDE * cols), jnp.bfloat16),
            pltpu.VMEM((WIDE * pairs, cols), jnp.bfloat16),
            pltpu.VMEM((WIDE * pairs, cols), jnp.bfloat16),
            pltpu.VMEM((all_alpha, WIDE * pairs), jnp.bfloat16),
            pltpu.VMEM((all_alpha, WIDE * pairs), jnp.bfloat16),
            pltpu.VMEM((all_alpha, cols), jnp.float32),
            pltpu.VMEM((n_alpha, rows, cols), jnp.bfloat16),
            pltpu.VMEM((n_alpha - 1, rows, cols), jnp.bfloat16),
            pltpu.SemaphoreType.DMA((6,)),
            pltpu.SemaphoreType.DMA((n_beta - 1,)),
            pltpu.SemaphoreType.DMA((n_beta - 1,)),
            pltpu.SemaphoreType.DMA((n_alpha - 1,)),
            pltpu.SemaphoreType.DMA((n_alpha - 1,)),
        ],
        compiler_params=pltpu.CompilerParams(
            collective_id=0, has_side_effects=True, vmem_limit_bytes=32 * 1024 * 1024
        ),
    )(*operands)


def solution(mesh):
    placed = (
        P("alpha", "beta"),
        P(),
        P(None, "beta"),
        P(None, "beta"),
        P("alpha", None),
        P("alpha", None),
    )
    return jax.shard_map(
        on_device, mesh=mesh, in_specs=placed, out_specs=P("alpha", "beta"), check_vma=False
    )
```

```python
import functools

import jax
import jax.numpy as jnp
from jax import lax
from jax.experimental import pallas as pl
from jax.experimental.pallas import tpu as pltpu
from jax.sharding import PartitionSpec as P

MESH = pl.DeviceIdType.MESH
LANES = 128
ROWS = 16
WIDE = 4


def spread_gather(values, lanes):
    numbers = lax.GatherDimensionNumbers(
        offset_dims=(),
        collapsed_slice_dims=(1,),
        start_index_map=(1,),
        operand_batching_dims=(0,),
        start_indices_batching_dims=(0,),
    )
    return lax.gather(
        values,
        lanes[:, :, None],
        numbers,
        slice_sizes=(1, 1),
        mode=lax.GatherScatterMode.PROMISE_IN_BOUNDS,
    )


def kernel(
    n_alpha,
    n_beta,
    coeffs_hbm,
    integrals_hbm,
    source_hbm,
    sign_b_hbm,
    target_hbm,
    sign_a_hbm,
    out_ref,
    integrals_ref,
    source_ref,
    sign_b_ref,
    target_ref,
    sign_a_ref,
    target_flat,
    sign_a_flat,
    gathered,
    spread,
    lane_ref,
    slot_ref,
    sign_ref,
    base,
    excited_0,
    excited_1,
    mixed_0,
    mixed_1,
    table_0,
    table_1,
    total,
    outgoing,
    incoming,
    load_sem,
    gather_send,
    gather_recv,
    sum_send,
    sum_recv,
):
    rows, cols = coeffs_hbm.shape
    pairs = integrals_hbm.shape[0]
    all_alpha = rows * n_alpha
    ia = lax.axis_index("alpha")
    ib = lax.axis_index("beta")

    sets = rows // WIDE

    barrier = pltpu.get_barrier_semaphore()
    for d in range(1, n_beta):
        pl.semaphore_signal(
            barrier, inc=1, device_id=(ia, lax.rem(ib + d, n_beta)), device_id_type=MESH
        )
    for d in range(1, n_alpha):
        pl.semaphore_signal(
            barrier, inc=1, device_id=(lax.rem(ia + d, n_alpha), ib), device_id_type=MESH
        )
    loads = [
        pltpu.make_async_copy(src, dst, load_sem.at[i])
        for i, (src, dst) in enumerate(
            (
                (coeffs_hbm, gathered.at[0]),
                (source_hbm, source_ref),
                (sign_b_hbm, sign_b_ref),
                (target_hbm, target_ref),
                (sign_a_hbm, sign_a_ref),
                (integrals_hbm, integrals_ref),
            )
        )
    ]
    for load in loads:
        load.start()
    pl.semaphore_wait(barrier, n_beta + n_alpha - 2)

    gather_copies = []
    for d in range(1, n_beta):
        copy = pltpu.make_async_remote_copy(
            src_ref=coeffs_hbm,
            dst_ref=gathered.at[d],
            send_sem=gather_send.at[d - 1],
            recv_sem=gather_recv.at[d - 1],
            device_id=(ia, lax.rem(ib + d, n_beta)),
            device_id_type=MESH,
        )
        copy.start()
        gather_copies.append(copy)

    loads[0].wait()
    loads[1].wait()
    source = source_ref[...]
    block = source // LANES
    lane_ref[...] = (source - block * LANES).astype(jnp.int16)
    slot = ib - block
    slot_ref[...] = jnp.where(slot < 0, slot + n_beta, slot).astype(jnp.int16)

    def spread_rows(d):
        for a in range(rows):
            spread[d, a] = jnp.broadcast_to(
                gathered[d, a : a + 1, :].astype(jnp.float32), (ROWS, LANES)
            ).astype(jnp.bfloat16)

    spread_rows(0)

    groups = pairs // ROWS
    together = max(n for n in range(1, 6) if groups % n == 0)

    def excite_own(step, carry):
        for u in range(together):
            at = pl.ds(pl.multiple_of((step * together + u) * ROWS, ROWS), ROWS)
            lane = lane_ref[at, :]
            for a in range(rows):
                base[a % sets, at, (a // sets) * cols : (a // sets + 1) * cols] = spread_gather(
                    spread[0, a], lane
                )
        return carry

    lax.fori_loop(0, groups // together, excite_own, 0)

    loads[2].wait()
    sign_ref[...] = sign_b_ref[...].astype(jnp.float32).astype(jnp.bfloat16)
    total[...] = jnp.zeros_like(total)
    for load in loads[3:]:
        load.wait()
    for src, dst in ((target_ref, target_flat), (sign_a_ref, sign_a_flat)):
        dst[...] = jnp.concatenate(
            [src[i * sets : (i + 1) * sets, :] for i in range(WIDE)], axis=1
        )
    for copy in gather_copies:
        copy.wait()
    for d in range(1, n_beta):
        spread_rows(d)

    def excite_group(p, out, at):
        lane = lane_ref[at, :]
        slot = slot_ref[at, :]
        sign = sign_ref[at, :]
        masks = [slot == jnp.int16(d) for d in range(n_beta)]
        for i in range(WIDE):
            value = base[p, at, i * cols : (i + 1) * cols]
            for d in range(1, n_beta):
                value = jnp.where(masks[d], spread_gather(spread[d, i * sets + p], lane), value)
            out[at, i * cols : (i + 1) * cols] = value * sign

    def excite(p, out, first, last):
        for g in range(first, last):
            excite_group(p, out, slice(g * ROWS, (g + 1) * ROWS))

    def contract(src, out):
        mixed = jnp.dot(
            integrals_ref[...], src[...], preferred_element_type=jnp.float32
        ).astype(jnp.bfloat16)
        for i in range(WIDE):
            out[i * pairs : (i + 1) * pairs, :] = mixed[:, i * cols : (i + 1) * cols]

    iota = lax.broadcasted_iota(jnp.int32, (ROWS, WIDE * pairs), 0)

    def build(p, out):
        row = pl.ds(p, 1)
        shape = (ROWS, WIDE * pairs)
        targets = (jnp.broadcast_to(target_flat[row, :], shape) - iota).astype(jnp.int16)
        signs = (
            jnp.broadcast_to(sign_a_flat[row, :], shape).astype(jnp.float32).astype(jnp.bfloat16)
        )
        zero = jnp.zeros_like(signs)
        for k in range(all_alpha // ROWS):
            out[k * ROWS : (k + 1) * ROWS, :] = jnp.where(
                targets == jnp.int16(k * ROWS), signs, zero
            )

    def scatter(table, mixed):
        total[...] += jnp.dot(table[...], mixed[...], preferred_element_type=jnp.float32)

    def stages(p, here, there, mixed, mixed_next, table, table_next):
        contract(there, mixed_next)
        excite(p + 2, here, 0, groups // 2)
        build(p + 1, table_next)
        scatter(table, mixed)
        excite(p + 2, here, groups // 2, groups)

    excite(0, excited_0, 0, groups)
    contract(excited_0, mixed_0)
    build(0, table_0)
    excite(1, excited_1, 0, groups)

    def step(s, carry):
        p = 2 * s
        stages(p, excited_0, excited_1, mixed_0, mixed_1, table_0, table_1)
        stages(p + 1, excited_1, excited_0, mixed_1, mixed_0, table_1, table_0)
        return carry

    lax.fori_loop(0, sets // 2 - 1, step, 0)
    contract(excited_1, mixed_1)
    build(sets - 1, table_1)
    scatter(table_0, mixed_0)
    scatter(table_1, mixed_1)

    for i in range(n_alpha):
        outgoing[i] = total[i * rows : (i + 1) * rows, :].astype(jnp.bfloat16)
    sum_copies = []
    for d in range(1, n_alpha):
        to = lax.rem(ia + d, n_alpha)
        copy = pltpu.make_async_remote_copy(
            src_ref=outgoing.at[to],
            dst_ref=incoming.at[d - 1],
            send_sem=sum_send.at[d - 1],
            recv_sem=sum_recv.at[d - 1],
            device_id=(to, ib),
            device_id_type=MESH,
        )
        copy.start()
        sum_copies.append(copy)
    result = total[pl.ds(pl.multiple_of(ia * rows, rows), rows), :]
    for d in range(1, n_alpha):
        sum_copies[d - 1].wait()
        result = result + incoming[d - 1].astype(jnp.float32)
    out_ref[...] = result


def on_device(coeffs, integrals, source_beta, sign_beta, target_alpha, sign_alpha):
    n_alpha = lax.axis_size("alpha")
    n_beta = lax.axis_size("beta")
    rows, cols = coeffs.shape
    pairs = integrals.shape[0]
    all_alpha = rows * n_alpha
    operands = [
        pltpu.with_memory_space_constraint(array, pltpu.HBM)
        for array in (coeffs, integrals, source_beta, sign_beta, target_alpha, sign_alpha)
    ]
    return pl.pallas_call(
        functools.partial(kernel, n_alpha, n_beta),
        out_shape=jax.ShapeDtypeStruct((rows, cols), jnp.float32),
        in_specs=[pl.BlockSpec(memory_space=pltpu.HBM)] * 6,
        out_specs=pl.BlockSpec(memory_space=pltpu.VMEM),
        scratch_shapes=[
            pltpu.VMEM((pairs, pairs), jnp.bfloat16),
            pltpu.VMEM((pairs, cols), jnp.int32),
            pltpu.VMEM((pairs, cols), jnp.int32),
            pltpu.VMEM((rows, pairs), jnp.int32),
            pltpu.VMEM((rows, pairs), jnp.int32),
            pltpu.VMEM((rows // WIDE, WIDE * pairs), jnp.int32),
            pltpu.VMEM((rows // WIDE, WIDE * pairs), jnp.int32),
            pltpu.VMEM((n_beta, rows, cols), jnp.bfloat16),
            pltpu.VMEM((n_beta, rows, ROWS, LANES), jnp.bfloat16),
            pltpu.VMEM((pairs, cols), jnp.int16),
            pltpu.VMEM((pairs, cols), jnp.int16),
            pltpu.VMEM((pairs, cols), jnp.bfloat16),
            pltpu.VMEM((rows // WIDE, pairs, WIDE * cols), jnp.bfloat16),
            pltpu.VMEM((pairs, WIDE * cols), jnp.bfloat16),
            pltpu.VMEM((pairs, WIDE * cols), jnp.bfloat16),
            pltpu.VMEM((WIDE * pairs, cols), jnp.bfloat16),
            pltpu.VMEM((WIDE * pairs, cols), jnp.bfloat16),
            pltpu.VMEM((all_alpha, WIDE * pairs), jnp.bfloat16),
            pltpu.VMEM((all_alpha, WIDE * pairs), jnp.bfloat16),
            pltpu.VMEM((all_alpha, cols), jnp.float32),
            pltpu.VMEM((n_alpha, rows, cols), jnp.bfloat16),
            pltpu.VMEM((n_alpha - 1, rows, cols), jnp.bfloat16),
            pltpu.SemaphoreType.DMA((6,)),
            pltpu.SemaphoreType.DMA((n_beta - 1,)),
            pltpu.SemaphoreType.DMA((n_beta - 1,)),
            pltpu.SemaphoreType.DMA((n_alpha - 1,)),
            pltpu.SemaphoreType.DMA((n_alpha - 1,)),
        ],
        compiler_params=pltpu.CompilerParams(
            collective_id=0, has_side_effects=True, vmem_limit_bytes=32 * 1024 * 1024
        ),
    )(*operands)


def solution(mesh):
    placed = (
        P("alpha", "beta"),
        P(),
        P(None, "beta"),
        P(None, "beta"),
        P("alpha", None),
        P("alpha", None),
    )
    return jax.shard_map(
        on_device, mesh=mesh, in_specs=placed, out_specs=P("alpha", "beta"), check_vma=False
    )
```

```python
import functools

import jax
import jax.numpy as jnp
from jax import lax
from jax.experimental import pallas as pl
from jax.experimental.pallas import tpu as pltpu
from jax.sharding import PartitionSpec as P

MESH = pl.DeviceIdType.MESH
LANES = 128
ROWS = 16
WIDE = 2


def spread_gather(values, lanes):
    numbers = lax.GatherDimensionNumbers(
        offset_dims=(),
        collapsed_slice_dims=(1,),
        start_index_map=(1,),
        operand_batching_dims=(0,),
        start_indices_batching_dims=(0,),
    )
    return lax.gather(
        values,
        lanes[:, :, None],
        numbers,
        slice_sizes=(1, 1),
        mode=lax.GatherScatterMode.PROMISE_IN_BOUNDS,
    )


def kernel(
    n_alpha,
    n_beta,
    coeffs_hbm,
    integrals_hbm,
    source_hbm,
    sign_b_hbm,
    target_hbm,
    sign_a_hbm,
    out_ref,
    integrals_ref,
    source_ref,
    sign_b_ref,
    target_ref,
    sign_a_ref,
    target_flat,
    sign_a_flat,
    gathered,
    spread,
    lane_ref,
    slot_ref,
    sign_ref,
    base,
    excited_0,
    excited_1,
    mixed_0,
    mixed_1,
    table_0,
    table_1,
    total,
    outgoing,
    incoming,
    load_sem,
    gather_send,
    gather_recv,
    sum_send,
    sum_recv,
):
    rows, cols = coeffs_hbm.shape
    pairs = integrals_hbm.shape[0]
    all_alpha = rows * n_alpha
    ia = lax.axis_index("alpha")
    ib = lax.axis_index("beta")

    sets = rows // WIDE

    barrier = pltpu.get_barrier_semaphore()
    for d in range(1, n_beta):
        pl.semaphore_signal(
            barrier, inc=1, device_id=(ia, lax.rem(ib + d, n_beta)), device_id_type=MESH
        )
    for d in range(1, n_alpha):
        pl.semaphore_signal(
            barrier, inc=1, device_id=(lax.rem(ia + d, n_alpha), ib), device_id_type=MESH
        )
    loads = [
        pltpu.make_async_copy(src, dst, load_sem.at[i])
        for i, (src, dst) in enumerate(
            (
                (coeffs_hbm, gathered.at[0]),
                (source_hbm, source_ref),
                (sign_b_hbm, sign_b_ref),
                (target_hbm, target_ref),
                (sign_a_hbm, sign_a_ref),
                (integrals_hbm, integrals_ref),
            )
        )
    ]
    for load in loads:
        load.start()
    pl.semaphore_wait(barrier, n_beta + n_alpha - 2)

    gather_copies = []
    for d in range(1, n_beta):
        copy = pltpu.make_async_remote_copy(
            src_ref=coeffs_hbm,
            dst_ref=gathered.at[d],
            send_sem=gather_send.at[d - 1],
            recv_sem=gather_recv.at[d - 1],
            device_id=(ia, lax.rem(ib + d, n_beta)),
            device_id_type=MESH,
        )
        copy.start()
        gather_copies.append(copy)

    loads[0].wait()
    loads[1].wait()
    source = source_ref[...]
    block = source // LANES
    lane_ref[...] = (source - block * LANES).astype(jnp.int16)
    slot = ib - block
    slot_ref[...] = jnp.where(slot < 0, slot + n_beta, slot).astype(jnp.int16)

    def spread_rows(d):
        for a in range(rows):
            spread[d, a] = jnp.broadcast_to(
                gathered[d, a : a + 1, :].astype(jnp.float32), (ROWS, LANES)
            ).astype(jnp.bfloat16)

    spread_rows(0)

    groups = pairs // ROWS
    together = max(n for n in range(1, 26) if groups % n == 0)

    def excite_own(step, carry):
        for u in range(together):
            at = pl.ds(pl.multiple_of((step * together + u) * ROWS, ROWS), ROWS)
            lane = lane_ref[at, :]
            for a in range(rows):
                base[a % sets, at, (a // sets) * cols : (a // sets + 1) * cols] = spread_gather(
                    spread[0, a], lane
                )
        return carry

    lax.fori_loop(0, groups // together, excite_own, 0)

    loads[2].wait()
    sign_ref[...] = sign_b_ref[...].astype(jnp.float32).astype(jnp.bfloat16)
    total[...] = jnp.zeros_like(total)
    for load in loads[3:]:
        load.wait()
    for src, dst in ((target_ref, target_flat), (sign_a_ref, sign_a_flat)):
        dst[...] = jnp.concatenate(
            [src[i * sets : (i + 1) * sets, :] for i in range(WIDE)], axis=1
        )
    for copy in gather_copies:
        copy.wait()
    for d in range(1, n_beta):
        spread_rows(d)

    def excite_group(p, out, at):
        lane = lane_ref[at, :]
        slot = slot_ref[at, :]
        sign = sign_ref[at, :]
        masks = [slot == jnp.int16(d) for d in range(n_beta)]
        for i in range(WIDE):
            value = base[p, at, i * cols : (i + 1) * cols]
            for d in range(1, n_beta):
                value = jnp.where(masks[d], spread_gather(spread[d, i * sets + p], lane), value)
            out[at, i * cols : (i + 1) * cols] = value * sign

    def excite(p, out, first, last):
        for g in range(first, last):
            excite_group(p, out, slice(g * ROWS, (g + 1) * ROWS))

    def contract(src, out):
        mixed = jnp.dot(
            integrals_ref[...], src[...], preferred_element_type=jnp.float32
        ).astype(jnp.bfloat16)
        for i in range(WIDE):
            out[i * pairs : (i + 1) * pairs, :] = mixed[:, i * cols : (i + 1) * cols]

    iota = lax.broadcasted_iota(jnp.int32, (ROWS, WIDE * pairs), 0)

    def build(p, out):
        row = pl.ds(p, 1)
        shape = (ROWS, WIDE * pairs)
        targets = (jnp.broadcast_to(target_flat[row, :], shape) - iota).astype(jnp.int16)
        signs = (
            jnp.broadcast_to(sign_a_flat[row, :], shape).astype(jnp.float32).astype(jnp.bfloat16)
        )
        zero = jnp.zeros_like(signs)
        for k in range(all_alpha // ROWS):
            out[k * ROWS : (k + 1) * ROWS, :] = jnp.where(
                targets == jnp.int16(k * ROWS), signs, zero
            )

    def scatter(table, mixed):
        total[...] += jnp.dot(table[...], mixed[...], preferred_element_type=jnp.float32)

    def stages(p, here, there, mixed, mixed_next, table, table_next):
        contract(there, mixed_next)
        excite(p + 2, here, 0, groups // 2)
        build(p + 1, table_next)
        scatter(table, mixed)
        excite(p + 2, here, groups // 2, groups)

    excite(0, excited_0, 0, groups)
    contract(excited_0, mixed_0)
    build(0, table_0)
    excite(1, excited_1, 0, groups)

    def step(s, carry):
        p = 2 * s
        stages(p, excited_0, excited_1, mixed_0, mixed_1, table_0, table_1)
        stages(p + 1, excited_1, excited_0, mixed_1, mixed_0, table_1, table_0)
        return carry

    lax.fori_loop(0, sets // 2 - 1, step, 0)
    contract(excited_1, mixed_1)
    build(sets - 1, table_1)
    scatter(table_0, mixed_0)
    scatter(table_1, mixed_1)

    for i in range(n_alpha):
        outgoing[i] = total[i * rows : (i + 1) * rows, :].astype(jnp.bfloat16)
    sum_copies = []
    for d in range(1, n_alpha):
        to = lax.rem(ia + d, n_alpha)
        copy = pltpu.make_async_remote_copy(
            src_ref=outgoing.at[to],
            dst_ref=incoming.at[d - 1],
            send_sem=sum_send.at[d - 1],
            recv_sem=sum_recv.at[d - 1],
            device_id=(to, ib),
            device_id_type=MESH,
        )
        copy.start()
        sum_copies.append(copy)
    result = total[pl.ds(pl.multiple_of(ia * rows, rows), rows), :]
    for d in range(1, n_alpha):
        sum_copies[d - 1].wait()
        result = result + incoming[d - 1].astype(jnp.float32)
    out_ref[...] = result


def on_device(coeffs, integrals, source_beta, sign_beta, target_alpha, sign_alpha):
    n_alpha = lax.axis_size("alpha")
    n_beta = lax.axis_size("beta")
    rows, cols = coeffs.shape
    pairs = integrals.shape[0]
    all_alpha = rows * n_alpha
    operands = [
        pltpu.with_memory_space_constraint(array, pltpu.HBM)
        for array in (coeffs, integrals, source_beta, sign_beta, target_alpha, sign_alpha)
    ]
    return pl.pallas_call(
        functools.partial(kernel, n_alpha, n_beta),
        out_shape=jax.ShapeDtypeStruct((rows, cols), jnp.float32),
        in_specs=[pl.BlockSpec(memory_space=pltpu.HBM)] * 6,
        out_specs=pl.BlockSpec(memory_space=pltpu.VMEM),
        scratch_shapes=[
            pltpu.VMEM((pairs, pairs), jnp.bfloat16),
            pltpu.VMEM((pairs, cols), jnp.int32),
            pltpu.VMEM((pairs, cols), jnp.int32),
            pltpu.VMEM((rows, pairs), jnp.int32),
            pltpu.VMEM((rows, pairs), jnp.int32),
            pltpu.VMEM((rows // WIDE, WIDE * pairs), jnp.int32),
            pltpu.VMEM((rows // WIDE, WIDE * pairs), jnp.int32),
            pltpu.VMEM((n_beta, rows, cols), jnp.bfloat16),
            pltpu.VMEM((n_beta, rows, ROWS, LANES), jnp.bfloat16),
            pltpu.VMEM((pairs, cols), jnp.int16),
            pltpu.VMEM((pairs, cols), jnp.int16),
            pltpu.VMEM((pairs, cols), jnp.bfloat16),
            pltpu.VMEM((rows // WIDE, pairs, WIDE * cols), jnp.bfloat16),
            pltpu.VMEM((pairs, WIDE * cols), jnp.bfloat16),
            pltpu.VMEM((pairs, WIDE * cols), jnp.bfloat16),
            pltpu.VMEM((WIDE * pairs, cols), jnp.bfloat16),
            pltpu.VMEM((WIDE * pairs, cols), jnp.bfloat16),
            pltpu.VMEM((all_alpha, WIDE * pairs), jnp.bfloat16),
            pltpu.VMEM((all_alpha, WIDE * pairs), jnp.bfloat16),
            pltpu.VMEM((all_alpha, cols), jnp.float32),
            pltpu.VMEM((n_alpha, rows, cols), jnp.bfloat16),
            pltpu.VMEM((n_alpha - 1, rows, cols), jnp.bfloat16),
            pltpu.SemaphoreType.DMA((6,)),
            pltpu.SemaphoreType.DMA((n_beta - 1,)),
            pltpu.SemaphoreType.DMA((n_beta - 1,)),
            pltpu.SemaphoreType.DMA((n_alpha - 1,)),
            pltpu.SemaphoreType.DMA((n_alpha - 1,)),
        ],
        compiler_params=pltpu.CompilerParams(
            collective_id=0, has_side_effects=True, vmem_limit_bytes=32 * 1024 * 1024
        ),
    )(*operands)


def solution(mesh):
    placed = (
        P("alpha", "beta"),
        P(),
        P(None, "beta"),
        P(None, "beta"),
        P("alpha", None),
        P("alpha", None),
    )
    return jax.shard_map(
        on_device, mesh=mesh, in_specs=placed, out_specs=P("alpha", "beta"), check_vma=False
    )
```

```python
import functools

import jax
import jax.numpy as jnp
from jax import lax
from jax.experimental import pallas as pl
from jax.experimental.pallas import tpu as pltpu
from jax.sharding import PartitionSpec as P

MESH = pl.DeviceIdType.MESH
LANES = 128
ROWS = 16
WIDE = 8


def spread_gather(values, lanes):
    numbers = lax.GatherDimensionNumbers(
        offset_dims=(),
        collapsed_slice_dims=(1,),
        start_index_map=(1,),
        operand_batching_dims=(0,),
        start_indices_batching_dims=(0,),
    )
    return lax.gather(
        values,
        lanes[:, :, None],
        numbers,
        slice_sizes=(1, 1),
        mode=lax.GatherScatterMode.PROMISE_IN_BOUNDS,
    )


def kernel(
    n_alpha,
    n_beta,
    coeffs_hbm,
    integrals_hbm,
    source_hbm,
    sign_b_hbm,
    target_hbm,
    sign_a_hbm,
    out_ref,
    integrals_ref,
    source_ref,
    sign_b_ref,
    target_ref,
    sign_a_ref,
    target_flat,
    sign_a_flat,
    gathered,
    spread,
    lane_ref,
    slot_ref,
    sign_ref,
    base,
    excited_0,
    excited_1,
    mixed_0,
    mixed_1,
    table_0,
    table_1,
    total,
    outgoing,
    incoming,
    load_sem,
    gather_send,
    gather_recv,
    sum_send,
    sum_recv,
):
    rows, cols = coeffs_hbm.shape
    pairs = integrals_hbm.shape[0]
    all_alpha = rows * n_alpha
    ia = lax.axis_index("alpha")
    ib = lax.axis_index("beta")

    sets = rows // WIDE

    barrier = pltpu.get_barrier_semaphore()
    for d in range(1, n_beta):
        pl.semaphore_signal(
            barrier, inc=1, device_id=(ia, lax.rem(ib + d, n_beta)), device_id_type=MESH
        )
    for d in range(1, n_alpha):
        pl.semaphore_signal(
            barrier, inc=1, device_id=(lax.rem(ia + d, n_alpha), ib), device_id_type=MESH
        )
    loads = [
        pltpu.make_async_copy(src, dst, load_sem.at[i])
        for i, (src, dst) in enumerate(
            (
                (coeffs_hbm, gathered.at[0]),
                (source_hbm, source_ref),
                (sign_b_hbm, sign_b_ref),
                (target_hbm, target_ref),
                (sign_a_hbm, sign_a_ref),
                (integrals_hbm, integrals_ref),
            )
        )
    ]
    for load in loads:
        load.start()
    pl.semaphore_wait(barrier, n_beta + n_alpha - 2)

    gather_copies = []
    for d in range(1, n_beta):
        copy = pltpu.make_async_remote_copy(
            src_ref=coeffs_hbm,
            dst_ref=gathered.at[d],
            send_sem=gather_send.at[d - 1],
            recv_sem=gather_recv.at[d - 1],
            device_id=(ia, lax.rem(ib + d, n_beta)),
            device_id_type=MESH,
        )
        copy.start()
        gather_copies.append(copy)

    loads[0].wait()
    loads[1].wait()
    source = source_ref[...]
    block = source // LANES
    lane_ref[...] = (source - block * LANES).astype(jnp.int16)
    slot = ib - block
    slot_ref[...] = jnp.where(slot < 0, slot + n_beta, slot).astype(jnp.int16)

    def spread_rows(d):
        for a in range(rows):
            spread[d, a] = jnp.broadcast_to(
                gathered[d, a : a + 1, :].astype(jnp.float32), (ROWS, LANES)
            ).astype(jnp.bfloat16)

    spread_rows(0)

    groups = pairs // ROWS
    together = max(n for n in range(1, 6) if groups % n == 0)

    def excite_own(step, carry):
        for u in range(together):
            at = pl.ds(pl.multiple_of((step * together + u) * ROWS, ROWS), ROWS)
            lane = lane_ref[at, :]
            for a in range(rows):
                base[a % sets, at, (a // sets) * cols : (a // sets + 1) * cols] = spread_gather(
                    spread[0, a], lane
                )
        return carry

    lax.fori_loop(0, groups // together, excite_own, 0)

    loads[2].wait()
    sign_ref[...] = sign_b_ref[...].astype(jnp.float32).astype(jnp.bfloat16)
    total[...] = jnp.zeros_like(total)
    for load in loads[3:]:
        load.wait()
    for src, dst in ((target_ref, target_flat), (sign_a_ref, sign_a_flat)):
        dst[...] = jnp.concatenate(
            [src[i * sets : (i + 1) * sets, :] for i in range(WIDE)], axis=1
        )
    for copy in gather_copies:
        copy.wait()
    for d in range(1, n_beta):
        spread_rows(d)

    def excite_group(p, out, at):
        lane = lane_ref[at, :]
        slot = slot_ref[at, :]
        sign = sign_ref[at, :]
        masks = [slot == jnp.int16(d) for d in range(n_beta)]
        for i in range(WIDE):
            value = base[p, at, i * cols : (i + 1) * cols]
            for d in range(1, n_beta):
                value = jnp.where(masks[d], spread_gather(spread[d, i * sets + p], lane), value)
            out[at, i * cols : (i + 1) * cols] = value * sign

    def excite(p, out, first, last):
        for g in range(first, last):
            excite_group(p, out, slice(g * ROWS, (g + 1) * ROWS))

    def contract(src, out):
        mixed = jnp.dot(
            integrals_ref[...], src[...], preferred_element_type=jnp.float32
        ).astype(jnp.bfloat16)
        for i in range(WIDE):
            out[i * pairs : (i + 1) * pairs, :] = mixed[:, i * cols : (i + 1) * cols]

    iota = lax.broadcasted_iota(jnp.int32, (ROWS, WIDE * pairs), 0)

    def build(p, out):
        row = pl.ds(p, 1)
        shape = (ROWS, WIDE * pairs)
        targets = (jnp.broadcast_to(target_flat[row, :], shape) - iota).astype(jnp.int16)
        signs = (
            jnp.broadcast_to(sign_a_flat[row, :], shape).astype(jnp.float32).astype(jnp.bfloat16)
        )
        zero = jnp.zeros_like(signs)
        for k in range(all_alpha // ROWS):
            out[k * ROWS : (k + 1) * ROWS, :] = jnp.where(
                targets == jnp.int16(k * ROWS), signs, zero
            )

    def scatter(table, mixed):
        total[...] += jnp.dot(table[...], mixed[...], preferred_element_type=jnp.float32)

    def stages(p, here, there, mixed, mixed_next, table, table_next):
        contract(there, mixed_next)
        excite(p + 2, here, 0, groups // 2)
        build(p + 1, table_next)
        scatter(table, mixed)
        excite(p + 2, here, groups // 2, groups)

    excite(0, excited_0, 0, groups)
    contract(excited_0, mixed_0)
    build(0, table_0)
    excite(1, excited_1, 0, groups)

    def step(s, carry):
        p = 2 * s
        stages(p, excited_0, excited_1, mixed_0, mixed_1, table_0, table_1)
        stages(p + 1, excited_1, excited_0, mixed_1, mixed_0, table_1, table_0)
        return carry

    lax.fori_loop(0, sets // 2 - 1, step, 0)
    contract(excited_1, mixed_1)
    build(sets - 1, table_1)
    scatter(table_0, mixed_0)
    scatter(table_1, mixed_1)

    for i in range(n_alpha):
        outgoing[i] = total[i * rows : (i + 1) * rows, :].astype(jnp.bfloat16)
    sum_copies = []
    for d in range(1, n_alpha):
        to = lax.rem(ia + d, n_alpha)
        copy = pltpu.make_async_remote_copy(
            src_ref=outgoing.at[to],
            dst_ref=incoming.at[d - 1],
            send_sem=sum_send.at[d - 1],
            recv_sem=sum_recv.at[d - 1],
            device_id=(to, ib),
            device_id_type=MESH,
        )
        copy.start()
        sum_copies.append(copy)
    result = total[pl.ds(pl.multiple_of(ia * rows, rows), rows), :]
    for d in range(1, n_alpha):
        sum_copies[d - 1].wait()
        result = result + incoming[d - 1].astype(jnp.float32)
    out_ref[...] = result


def on_device(coeffs, integrals, source_beta, sign_beta, target_alpha, sign_alpha):
    n_alpha = lax.axis_size("alpha")
    n_beta = lax.axis_size("beta")
    rows, cols = coeffs.shape
    pairs = integrals.shape[0]
    all_alpha = rows * n_alpha
    operands = [
        pltpu.with_memory_space_constraint(array, pltpu.HBM)
        for array in (coeffs, integrals, source_beta, sign_beta, target_alpha, sign_alpha)
    ]
    return pl.pallas_call(
        functools.partial(kernel, n_alpha, n_beta),
        out_shape=jax.ShapeDtypeStruct((rows, cols), jnp.float32),
        in_specs=[pl.BlockSpec(memory_space=pltpu.HBM)] * 6,
        out_specs=pl.BlockSpec(memory_space=pltpu.VMEM),
        scratch_shapes=[
            pltpu.VMEM((pairs, pairs), jnp.bfloat16),
            pltpu.VMEM((pairs, cols), jnp.int32),
            pltpu.VMEM((pairs, cols), jnp.int32),
            pltpu.VMEM((rows, pairs), jnp.int32),
            pltpu.VMEM((rows, pairs), jnp.int32),
            pltpu.VMEM((rows // WIDE, WIDE * pairs), jnp.int32),
            pltpu.VMEM((rows // WIDE, WIDE * pairs), jnp.int32),
            pltpu.VMEM((n_beta, rows, cols), jnp.bfloat16),
            pltpu.VMEM((n_beta, rows, ROWS, LANES), jnp.bfloat16),
            pltpu.VMEM((pairs, cols), jnp.int16),
            pltpu.VMEM((pairs, cols), jnp.int16),
            pltpu.VMEM((pairs, cols), jnp.bfloat16),
            pltpu.VMEM((rows // WIDE, pairs, WIDE * cols), jnp.bfloat16),
            pltpu.VMEM((pairs, WIDE * cols), jnp.bfloat16),
            pltpu.VMEM((pairs, WIDE * cols), jnp.bfloat16),
            pltpu.VMEM((WIDE * pairs, cols), jnp.bfloat16),
            pltpu.VMEM((WIDE * pairs, cols), jnp.bfloat16),
            pltpu.VMEM((all_alpha, WIDE * pairs), jnp.bfloat16),
            pltpu.VMEM((all_alpha, WIDE * pairs), jnp.bfloat16),
            pltpu.VMEM((all_alpha, cols), jnp.float32),
            pltpu.VMEM((n_alpha, rows, cols), jnp.bfloat16),
            pltpu.VMEM((n_alpha - 1, rows, cols), jnp.bfloat16),
            pltpu.SemaphoreType.DMA((6,)),
            pltpu.SemaphoreType.DMA((n_beta - 1,)),
            pltpu.SemaphoreType.DMA((n_beta - 1,)),
            pltpu.SemaphoreType.DMA((n_alpha - 1,)),
            pltpu.SemaphoreType.DMA((n_alpha - 1,)),
        ],
        compiler_params=pltpu.CompilerParams(
            collective_id=0, has_side_effects=True, vmem_limit_bytes=32 * 1024 * 1024
        ),
    )(*operands)


def solution(mesh):
    placed = (
        P("alpha", "beta"),
        P(),
        P(None, "beta"),
        P(None, "beta"),
        P("alpha", None),
        P("alpha", None),
    )
    return jax.shard_map(
        on_device, mesh=mesh, in_specs=placed, out_specs=P("alpha", "beta"), check_vma=False
    )
```

```python
import functools

import jax
import jax.numpy as jnp
from jax import lax
from jax.experimental import pallas as pl
from jax.experimental.pallas import tpu as pltpu
from jax.sharding import PartitionSpec as P

MESH = pl.DeviceIdType.MESH
LANES = 128
ROWS = 16
WIDE = 4


def spread_gather(values, lanes):
    numbers = lax.GatherDimensionNumbers(
        offset_dims=(),
        collapsed_slice_dims=(1,),
        start_index_map=(1,),
        operand_batching_dims=(0,),
        start_indices_batching_dims=(0,),
    )
    return lax.gather(
        values,
        lanes[:, :, None],
        numbers,
        slice_sizes=(1, 1),
        mode=lax.GatherScatterMode.PROMISE_IN_BOUNDS,
    )


def kernel(
    n_alpha,
    n_beta,
    coeffs_hbm,
    integrals_hbm,
    source_hbm,
    sign_b_hbm,
    target_hbm,
    sign_a_hbm,
    out_ref,
    integrals_ref,
    source_ref,
    sign_b_ref,
    target_ref,
    sign_a_ref,
    target_flat,
    sign_a_flat,
    gathered,
    spread,
    lane_ref,
    slot_ref,
    sign_ref,
    base,
    excited_0,
    excited_1,
    mixed_0,
    mixed_1,
    table_0,
    table_1,
    total,
    outgoing,
    incoming,
    load_sem,
    gather_send,
    gather_recv,
    sum_send,
    sum_recv,
):
    rows, cols = coeffs_hbm.shape
    pairs = integrals_hbm.shape[0]
    all_alpha = rows * n_alpha
    ia = lax.axis_index("alpha")
    ib = lax.axis_index("beta")

    sets = rows // WIDE

    barrier = pltpu.get_barrier_semaphore()
    for d in range(1, n_beta):
        pl.semaphore_signal(
            barrier, inc=1, device_id=(ia, lax.rem(ib + d, n_beta)), device_id_type=MESH
        )
    for d in range(1, n_alpha):
        pl.semaphore_signal(
            barrier, inc=1, device_id=(lax.rem(ia + d, n_alpha), ib), device_id_type=MESH
        )
    loads = [
        pltpu.make_async_copy(src, dst, load_sem.at[i])
        for i, (src, dst) in enumerate(
            (
                (coeffs_hbm, gathered.at[0]),
                (source_hbm, source_ref),
                (sign_b_hbm, sign_b_ref),
                (target_hbm, target_ref),
                (sign_a_hbm, sign_a_ref),
                (integrals_hbm, integrals_ref),
            )
        )
    ]
    for load in loads:
        load.start()
    pl.semaphore_wait(barrier, n_beta + n_alpha - 2)

    gather_copies = []
    for d in range(1, n_beta):
        copy = pltpu.make_async_remote_copy(
            src_ref=coeffs_hbm,
            dst_ref=gathered.at[d],
            send_sem=gather_send.at[d - 1],
            recv_sem=gather_recv.at[d - 1],
            device_id=(ia, lax.rem(ib + d, n_beta)),
            device_id_type=MESH,
        )
        copy.start()
        gather_copies.append(copy)

    loads[0].wait()
    loads[1].wait()
    source = source_ref[...]
    block = source // LANES
    lane_ref[...] = (source - block * LANES).astype(jnp.int16)
    slot = ib - block
    slot_ref[...] = jnp.where(slot < 0, slot + n_beta, slot).astype(jnp.int16)

    def spread_rows(d):
        for a in range(rows):
            spread[d, a] = jnp.broadcast_to(
                gathered[d, a : a + 1, :].astype(jnp.float32), (ROWS, LANES)
            ).astype(jnp.bfloat16)

    spread_rows(0)

    groups = pairs // ROWS
    together = max(n for n in range(1, 6) if groups % n == 0)

    def excite_own(step, carry):
        for u in range(together):
            at = pl.ds(pl.multiple_of((step * together + u) * ROWS, ROWS), ROWS)
            lane = lane_ref[at, :]
            for a in range(rows):
                base[a % sets, at, (a // sets) * cols : (a // sets + 1) * cols] = spread_gather(
                    spread[0, a], lane
                )
        return carry

    lax.fori_loop(0, groups // together, excite_own, 0)

    loads[2].wait()
    sign_ref[...] = sign_b_ref[...].astype(jnp.float32).astype(jnp.bfloat16)
    total[...] = jnp.zeros_like(total)
    for load in loads[3:]:
        load.wait()
    for src, dst in ((target_ref, target_flat), (sign_a_ref, sign_a_flat)):
        dst[...] = jnp.concatenate(
            [src[i * sets : (i + 1) * sets, :] for i in range(WIDE)], axis=1
        )
    for copy in gather_copies:
        copy.wait()
    for d in range(1, n_beta):
        spread_rows(d)

    def excite_group(p, out, at):
        lane = lane_ref[at, :]
        slot = slot_ref[at, :]
        sign = sign_ref[at, :]
        masks = [slot == jnp.int16(d) for d in range(n_beta)]
        for i in range(WIDE):
            value = base[p, at, i * cols : (i + 1) * cols]
            for d in range(1, n_beta):
                value = jnp.where(masks[d], spread_gather(spread[d, i * sets + p], lane), value)
            out[at, i * cols : (i + 1) * cols] = value * sign

    def excite(p, out, first, last):
        for g in range(first, last):
            excite_group(p, out, slice(g * ROWS, (g + 1) * ROWS))

    def contract(src, out):
        mixed = jnp.dot(
            integrals_ref[...], src[...], preferred_element_type=jnp.float32
        ).astype(jnp.bfloat16)
        for i in range(WIDE):
            out[i * pairs : (i + 1) * pairs, :] = mixed[:, i * cols : (i + 1) * cols]

    iota = lax.broadcasted_iota(jnp.int32, (ROWS, WIDE * pairs), 0)

    def build(p, out):
        row = pl.ds(p, 1)
        shape = (ROWS, WIDE * pairs)
        targets = (jnp.broadcast_to(target_flat[row, :], shape) - iota).astype(jnp.int16)
        signs = (
            jnp.broadcast_to(sign_a_flat[row, :], shape).astype(jnp.float32).astype(jnp.bfloat16)
        )
        zero = jnp.zeros_like(signs)
        for k in range(all_alpha // ROWS):
            out[k * ROWS : (k + 1) * ROWS, :] = jnp.where(
                targets == jnp.int16(k * ROWS), signs, zero
            )

    def scatter(table, mixed):
        total[...] += jnp.dot(table[...], mixed[...], preferred_element_type=jnp.float32)

    def stages(p, here, there, mixed, mixed_next, table, table_next):
        contract(there, mixed_next)
        scatter(table, mixed)
        build(p + 1, table_next)
        excite(p + 2, here, 0, groups)

    excite(0, excited_0, 0, groups)
    contract(excited_0, mixed_0)
    build(0, table_0)
    excite(1, excited_1, 0, groups)

    def step(s, carry):
        p = 2 * s
        stages(p, excited_0, excited_1, mixed_0, mixed_1, table_0, table_1)
        stages(p + 1, excited_1, excited_0, mixed_1, mixed_0, table_1, table_0)
        return carry

    lax.fori_loop(0, sets // 2 - 1, step, 0)
    build(sets - 1, table_1)
    contract(excited_1, mixed_1)
    scatter(table_0, mixed_0)
    scatter(table_1, mixed_1)

    for i in range(n_alpha):
        outgoing[i] = total[i * rows : (i + 1) * rows, :].astype(jnp.bfloat16)
    sum_copies = []
    for d in range(1, n_alpha):
        to = lax.rem(ia + d, n_alpha)
        copy = pltpu.make_async_remote_copy(
            src_ref=outgoing.at[to],
            dst_ref=incoming.at[d - 1],
            send_sem=sum_send.at[d - 1],
            recv_sem=sum_recv.at[d - 1],
            device_id=(to, ib),
            device_id_type=MESH,
        )
        copy.start()
        sum_copies.append(copy)
    result = total[pl.ds(pl.multiple_of(ia * rows, rows), rows), :]
    for d in range(1, n_alpha):
        sum_copies[d - 1].wait()
        result = result + incoming[d - 1].astype(jnp.float32)
    out_ref[...] = result


def on_device(coeffs, integrals, source_beta, sign_beta, target_alpha, sign_alpha):
    n_alpha = lax.axis_size("alpha")
    n_beta = lax.axis_size("beta")
    rows, cols = coeffs.shape
    pairs = integrals.shape[0]
    all_alpha = rows * n_alpha
    operands = [
        pltpu.with_memory_space_constraint(array, pltpu.HBM)
        for array in (coeffs, integrals, source_beta, sign_beta, target_alpha, sign_alpha)
    ]
    return pl.pallas_call(
        functools.partial(kernel, n_alpha, n_beta),
        out_shape=jax.ShapeDtypeStruct((rows, cols), jnp.float32),
        in_specs=[pl.BlockSpec(memory_space=pltpu.HBM)] * 6,
        out_specs=pl.BlockSpec(memory_space=pltpu.VMEM),
        scratch_shapes=[
            pltpu.VMEM((pairs, pairs), jnp.bfloat16),
            pltpu.VMEM((pairs, cols), jnp.int32),
            pltpu.VMEM((pairs, cols), jnp.int32),
            pltpu.VMEM((rows, pairs), jnp.int32),
            pltpu.VMEM((rows, pairs), jnp.int32),
            pltpu.VMEM((rows // WIDE, WIDE * pairs), jnp.int32),
            pltpu.VMEM((rows // WIDE, WIDE * pairs), jnp.int32),
            pltpu.VMEM((n_beta, rows, cols), jnp.bfloat16),
            pltpu.VMEM((n_beta, rows, ROWS, LANES), jnp.bfloat16),
            pltpu.VMEM((pairs, cols), jnp.int16),
            pltpu.VMEM((pairs, cols), jnp.int16),
            pltpu.VMEM((pairs, cols), jnp.bfloat16),
            pltpu.VMEM((rows // WIDE, pairs, WIDE * cols), jnp.bfloat16),
            pltpu.VMEM((pairs, WIDE * cols), jnp.bfloat16),
            pltpu.VMEM((pairs, WIDE * cols), jnp.bfloat16),
            pltpu.VMEM((WIDE * pairs, cols), jnp.bfloat16),
            pltpu.VMEM((WIDE * pairs, cols), jnp.bfloat16),
            pltpu.VMEM((all_alpha, WIDE * pairs), jnp.bfloat16),
            pltpu.VMEM((all_alpha, WIDE * pairs), jnp.bfloat16),
            pltpu.VMEM((all_alpha, cols), jnp.float32),
            pltpu.VMEM((n_alpha, rows, cols), jnp.bfloat16),
            pltpu.VMEM((n_alpha - 1, rows, cols), jnp.bfloat16),
            pltpu.SemaphoreType.DMA((6,)),
            pltpu.SemaphoreType.DMA((n_beta - 1,)),
            pltpu.SemaphoreType.DMA((n_beta - 1,)),
            pltpu.SemaphoreType.DMA((n_alpha - 1,)),
            pltpu.SemaphoreType.DMA((n_alpha - 1,)),
        ],
        compiler_params=pltpu.CompilerParams(
            collective_id=0, has_side_effects=True, vmem_limit_bytes=32 * 1024 * 1024
        ),
    )(*operands)


def solution(mesh):
    placed = (
        P("alpha", "beta"),
        P(),
        P(None, "beta"),
        P(None, "beta"),
        P("alpha", None),
        P("alpha", None),
    )
    return jax.shard_map(
        on_device, mesh=mesh, in_specs=placed, out_specs=P("alpha", "beta"), check_vma=False
    )
```
